32 devices in a mesh: groups: 2 (over x), tile: 16 (over z, y, core).
Axes of the slice: x: 2, y: 2, z: 4, core: 2. Of those that a mesh axis runs over, the one named last changes fastest.
Arguments:
- queries: bfloat16 [8, 768, 2560], P('groups', 'tile'), parts along dimension 0, may hold values from -60 to 60
- frame_kv: bfloat16 [8, 768, 2, 2560], P('groups', 'tile'), parts along dimension 0, may hold values from -7 to 7
- memory_kv: bfloat16 [8, 768, 2, 2560], P('groups', 'tile'), parts along dimension 0, may hold values from -6 to 6
- window_offsets: int32 [10], P('groups'), parts along dimension 0, may hold values from -3 to 3, as said below
- memory_frame: int32 [96, 5], P(('groups', 'tile')), parts along dimension 0, may hold values from 0 to 3
- memory_tile: int32 [96, 5], P(('groups', 'tile')), parts along dimension 0, may hold values from 0 to 47, as said below
Outputs:
- attended: bfloat16 [8, 768, 2560], P('groups', 'tile'), parts along dimension 0
The draws below stay inside these ranges and needn't reach their ends.
There are 2 independent parts, one for each index of `groups`. The reference program is written for one: setup_inputs(seed, part) draws one part's arguments, and reference() takes and returns one part's arrays. A program takes and returns all parts, laid end to end along the dimension named above; each array names one. Nothing has to cross between parts.
Inputs may be any that keep to these rules, and one draw needn't show every extreme that they name: `window_offsets`: the values are distinct and include -3, 0 and 3. `memory_tile`: for every device d, the 15 entries of rows d * 3 to d * 3 + 2 name tiles t whose values t // 3 are all different.
All inputs are finite; a program needn't handle non-finite values.
Results may differ from the reference program's by a relative error of at most 0.0033.
Values may be sent and summed in bfloat16 or wider, within the bound.
A program may use at most 256 MiB of HBM per device.

```python
import jax
import jax.numpy as jnp
from jax import lax

HEADS = 20
HEAD_DIM = 128
FRAMES = 4
TILE_TOK = 16
TPD = 3
RADIUS = 3
NBR = 5
MEMF = 4
TILES = 48
MEMK = 5


def pair_fields(key):
    row_count = TILES * TILE_TOK
    columns = HEADS * HEAD_DIM
    shape = (FRAMES, row_count, columns)
    key_query, key_keys, key_values = jax.random.split(jax.random.fold_in(key, 11), 3)
    query_field = 2.0 * jax.random.truncated_normal(key_query, -6.0, 6.0, shape)
    key_field = jax.random.truncated_normal(key_keys, -6.0, 6.0, shape)
    value_field = jax.random.truncated_normal(key_values, -6.0, 6.0, shape)
    return (query_field, jnp.stack([key_field, value_field], axis=2))


def draw_queries(key, part):
    return pair_fields(key)[0].astype(jnp.bfloat16)


def draw_frame_kv(key, part):
    return pair_fields(key)[1].astype(jnp.bfloat16)


def draw_window_offsets(key, part):
    between = jnp.concatenate([jnp.arange(-RADIUS + 1, 0), jnp.arange(1, RADIUS)]).astype(jnp.int32)
    shuffled = jax.random.permutation(jax.random.fold_in(key, 3), between.shape[0])
    chosen_extra = between[shuffled[:NBR - 3]]
    return jnp.concatenate([jnp.array([-RADIUS, 0, RADIUS], dtype=jnp.int32), chosen_extra]).astype(jnp.int32)


def memory_lists(key):
    processor_count = TILES // TPD
    per_device = TPD * MEMK
    key_center, key_noise, key_local, key_frame = jax.random.split(jax.random.fold_in(key, 5), 4)
    patch_midpoint = jax.random.randint(key_center, (), 0, processor_count)
    holder_numbers = jnp.arange(processor_count, dtype=jnp.int32)
    logit_increment = jnp.maximum(processor_count // 4 - jnp.abs(holder_numbers - patch_midpoint), 0)
    noise_perturbation = jax.random.randint(key_noise, (processor_count, processor_count), 0, processor_count)
    patch_ordering = (noise_perturbation + logit_increment[None, :]) * processor_count + holder_numbers[None, :]
    chosen = lax.top_k(patch_ordering, per_device)[0] % processor_count
    local_tile = jax.random.randint(key_local, (processor_count, per_device), 0, TPD)
    tiles = (chosen * TPD + local_tile).reshape(TILES, MEMK).astype(jnp.int32)
    video_moments = jax.random.randint(key_frame, (TILES, MEMK), 0, MEMF).astype(jnp.int32)
    return (video_moments, tiles)


def draw_memory_frame(key, part):
    return memory_lists(key)[0]


def draw_memory_tile(key, part):
    return memory_lists(key)[1]


def levels(rng, extent, shards, smallest, largest):
    def one(dim, parts):
        steps = jax.random.uniform(jax.random.fold_in(jax.random.fold_in(rng, 6), dim), (parts,), jnp.float32, smallest / len(shards), largest / len(shards))
        return jnp.repeat(jnp.exp(steps), extent[dim] // parts).reshape((-1,) + (1,) * (len(extent) - dim - 1))

    gain = one(*shards[0])
    for cut in shards[1:]:
        gain = gain * one(*cut)
    return gain


def scatter_about(rng, extent, spread, limit, pieces=(), kind=jnp.bfloat16):
    values = jax.random.normal(rng, extent, jnp.float32) * spread
    if len(pieces) > 0:
        values = levels(rng, extent, pieces, -0.22, 0.18) * values
    return jnp.clip(values, min=-limit, max=limit).astype(kind)


def setup_inputs(seed: int = 0, part: int = 0) -> dict:
    arg_keys = jax.random.split(jax.random.key(seed), 7)
    own_keys = jax.random.split(jax.random.fold_in(arg_keys[6], part), 7)
    return {
        "queries": draw_queries(jax.random.fold_in(jax.random.fold_in(arg_keys[6], part), 71), part),
        "frame_kv": draw_frame_kv(jax.random.fold_in(jax.random.fold_in(arg_keys[6], part), 71), part),
        "memory_kv": scatter_about(own_keys[2], (MEMF, TILES * TILE_TOK, 2, HEADS * HEAD_DIM), 1.0, 6.0, ((1, 16),)),
        "window_offsets": draw_window_offsets(jax.random.fold_in(jax.random.fold_in(arg_keys[6], part), 71), part),
        "memory_frame": draw_memory_frame(jax.random.fold_in(jax.random.fold_in(arg_keys[6], part), 71), part),
        "memory_tile": draw_memory_tile(jax.random.fold_in(jax.random.fold_in(arg_keys[6], part), 71), part),
    }


def reference(queries, frame_kv, memory_kv, window_offsets, memory_frame, memory_tile):
    video_moments = queries.shape[0]
    columns = queries.shape[2]
    head_count = columns // HEAD_DIM
    score_scale = HEAD_DIM ** -0.5
    frame_store = frame_kv.reshape(video_moments, TILES, TILE_TOK, 2, columns)
    memory_store = memory_kv.reshape(MEMF, TILES, TILE_TOK, 2, columns)

    def single_tile(tile_index):
        tile_queries = lax.dynamic_slice_in_dim(queries, tile_index * TILE_TOK, TILE_TOK, 1)
        neighbours = (tile_index + window_offsets).astype(jnp.int32)
        usable = (neighbours >= 0) & (neighbours < TILES)
        clipped_tiles = jnp.clip(neighbours, 0, TILES - 1).astype(jnp.int32)
        window = frame_store[:, clipped_tiles].reshape(video_moments * NBR * TILE_TOK, 2, columns)
        usable_window = jnp.broadcast_to(usable[None, :, None], (video_moments, NBR, TILE_TOK)).reshape(-1)
        memory_rows = memory_store[memory_frame[tile_index], memory_tile[tile_index]]
        memory_rows = memory_rows.reshape(MEMK * TILE_TOK, 2, columns)
        key_rows = jnp.concatenate([window, memory_rows], axis=0)
        usable_keys = jnp.concatenate([usable_window, jnp.ones((MEMK * TILE_TOK,), dtype=bool)])
        query_part = tile_queries.reshape(video_moments * TILE_TOK, head_count, HEAD_DIM).astype(jnp.float32)
        key_part = key_rows[:, 0].reshape(-1, head_count, HEAD_DIM).astype(jnp.float32)
        value_part = key_rows[:, 1].reshape(-1, head_count, HEAD_DIM).astype(jnp.float32)
        scores = jnp.einsum("qhd,khd->hqk", query_part, key_part) * score_scale
        scores = jnp.where(usable_keys[None, None, :], scores, -1e30)
        row_top = jnp.max(scores, axis=2, keepdims=True)
        exponent_terms = jnp.exp(scores - row_top)
        row_total = jnp.sum(exponent_terms, axis=2)
        weights = exponent_terms.astype(jnp.bfloat16)
        summed = jnp.einsum("hqk,khd->qhd", weights.astype(jnp.float32), value_part)
        attended = summed / jnp.transpose(row_total, (1, 0))[..., None]
        return attended.astype(jnp.bfloat16).reshape(video_moments, TILE_TOK, columns)

    final_output = lax.map(single_tile, jnp.arange(TILES, dtype=jnp.int32))
    return jnp.transpose(final_output, (1, 0, 2, 3)).reshape(video_moments, TILES * TILE_TOK, columns)
```

```python
import functools

import jax
import jax.numpy as jnp
from jax import lax
from jax.experimental import pallas as pl
from jax.experimental.pallas import tpu as pltpu
from jax.sharding import PartitionSpec as P

HEAD_DIM = 128
TILE_TOK = 16
TPD = 3
RADIUS = 3
CHUNKS = 5
OFF = -1e30


def kernel(
    n,
    wo_ref,
    mf_ref,
    mt_ref,
    q_ref,
    kv_ref,
    store_ref,
    out_ref,
    halo,
    mem_out,
    mem_in,
    req_out,
    req_in,
    req_now,
    bias,
    req_send,
    req_recv,
    local_sem,
    halo_send,
    halo_recv,
    mem_send,
    mem_recv,
):
    me = lax.axis_index("tile")
    heads = kv_ref.shape[0]
    frames = q_ref.shape[0]
    rows = TPD * TILE_TOK
    tokens = frames * rows
    listed = mt_ref.shape[1]
    per = heads // CHUNKS

    def peer_of(k):
        return lax.rem(me + k, n)

    barrier = pltpu.get_barrier_semaphore()

    @pl.loop(1, n)
    def _(k):
        pl.semaphore_signal(barrier, inc=1, device_id={"tile": peer_of(k)})

    row = lax.broadcasted_iota(jnp.int32, (n, 1, 128), 0)
    wanted = jnp.zeros((n, 1, 128), jnp.int32)
    for a in range(TPD):
        for j in range(listed):
            tile = mt_ref[a, j]
            slot = mf_ref[a, j] * TPD + lax.rem(tile, TPD)
            wanted = jnp.where(row == lax.div(tile, TPD), slot, wanted)
    req_out[...] = wanted

    pl.semaphore_wait(barrier, n - 1)

    def req_copy(k):
        return pltpu.make_async_remote_copy(
            src_ref=req_out.at[peer_of(k)],
            dst_ref=req_in.at[me],
            send_sem=req_send,
            recv_sem=req_recv,
            device_id={"tile": peer_of(k)},
        )

    @pl.loop(1, n)
    def _(k):
        req_copy(k).start()

    def halo_copy(side, c):
        part = pl.ds(c * per, per)
        return pltpu.make_async_remote_copy(
            src_ref=kv_ref.at[part],
            dst_ref=halo.at[side, part],
            send_sem=halo_send.at[side, c],
            recv_sem=halo_recv.at[side, c],
            device_id={"tile": lax.rem(me + 1, n) if side == 0 else lax.rem(me + n - 1, n)},
        )

    def send_halo(c):
        @pl.when(me < n - 1)
        def _():
            halo_copy(0, c).start()

        @pl.when(me > 0)
        def _():
            halo_copy(1, c).start()

    send_halo(0)

    column = lax.broadcasted_iota(jnp.int32, (TILE_TOK, 3 * tokens), 1)
    source = lax.div(column, tokens)
    local = lax.div(lax.rem(column, rows), TILE_TOK)
    span = local + jnp.where(source == 0, 0, jnp.where(source == 1, -TPD, TPD))
    there = span + me * TPD
    inside = (there >= 0) & (there < n * TPD)
    owner = lax.div(lax.broadcasted_iota(jnp.int32, (TILE_TOK, n * TILE_TOK), 1), TILE_TOK)
    for a in range(TPD):
        hit = jnp.zeros(span.shape, jnp.int32)
        for j in range(wo_ref.shape[0]):
            hit = jnp.where(span - a == wo_ref[j], 1, hit)
        near = jnp.where((hit == 1) & inside, 0.0, OFF)
        got = jnp.zeros(owner.shape, jnp.int32)
        for j in range(listed):
            got = jnp.where(owner == lax.div(mt_ref[a, j], TPD), 1, got)
        far = jnp.where(got == 1, 0.0, OFF)
        for f in range(frames):
            at = pl.ds(f * rows + a * TILE_TOK, TILE_TOK)
            bias[at, : 3 * tokens] = near
            bias[at, 3 * tokens :] = far

    @pl.when(me == 0)
    def _():
        @pl.loop(0, heads)
        def _(h):
            halo[0, h] = jnp.zeros(halo.shape[2:], halo.dtype)

    @pl.when(me == n - 1)
    def _():
        @pl.loop(0, heads)
        def _(h):
            halo[1, h] = jnp.zeros(halo.shape[2:], halo.dtype)

    pltpu.make_async_copy(
        req_in.at[pl.ds(0, n - 1)], req_in.at[pl.ds(0, n - 1)], req_recv
    ).wait()
    req_in[me] = req_out[me]
    to_scalar = pltpu.make_async_copy(req_in, req_now, local_sem)
    to_scalar.start()
    to_scalar.wait()

    def mem_copy(k, c):
        part = pl.ds(c * per, per)
        return pltpu.make_async_remote_copy(
            src_ref=mem_out.at[peer_of(k), part],
            dst_ref=mem_in.at[me, part],
            send_sem=mem_send,
            recv_sem=mem_recv.at[c],
            device_id={"tile": peer_of(k)},
        )

    for c in range(CHUNKS):
        part = pl.ds(c * per, per)
        if c > 0:
            send_halo(c)

        @pl.loop(1, n)
        def _(k):
            mem_out[peer_of(k), part] = store_ref[req_now[peer_of(k), 0, 0], part]
            mem_copy(k, c).start()

        mem_in[me, part] = store_ref[req_now[me, 0, 0], part]

    scale = HEAD_DIM**-0.5

    def one_head(h):
        at = pl.ds(pl.multiple_of(h * HEAD_DIM, HEAD_DIM), HEAD_DIM)
        q = q_ref[:, :, at].reshape(tokens, HEAD_DIM)
        pairs = [
            (kv_ref[h, 0], kv_ref[h, 1]),
            (halo[0, h, 0], halo[0, h, 1]),
            (halo[1, h, 0], halo[1, h, 1]),
            (
                mem_in[:, h, 0].reshape(n * TILE_TOK, HEAD_DIM),
                mem_in[:, h, 1].reshape(n * TILE_TOK, HEAD_DIM),
            ),
        ]
        keys = jnp.concatenate([k for k, _ in pairs], axis=0)
        values = jnp.concatenate([v for _, v in pairs], axis=0)
        scores = lax.dot_general(
            q, keys, (((1,), (1,)), ((), ())), preferred_element_type=jnp.float32
        )
        scores = scores * scale + bias[...]
        top = jnp.max(scores, axis=1, keepdims=True)
        terms = jnp.exp(scores - top)
        total = jnp.sum(terms, axis=1, keepdims=True)
        summed = jnp.dot(terms.astype(jnp.bfloat16), values, preferred_element_type=jnp.float32)
        out_ref[:, :, at] = (summed / total).astype(out_ref.dtype).reshape(frames, rows, HEAD_DIM)

    for c in range(CHUNKS):
        part = pl.ds(c * per, per)

        @pl.when(me > 0)
        def _():
            halo_copy(0, c).wait_recv()

        @pl.when(me < n - 1)
        def _():
            halo_copy(1, c).wait_recv()

        arrived = mem_in.at[pl.ds(0, n - 1), part]
        pltpu.make_async_copy(arrived, arrived, mem_recv.at[c]).wait()

        @pl.loop(c * per, (c + 1) * per)
        def _(h):
            one_head(h)

    for c in range(CHUNKS):

        @pl.when(me < n - 1)
        def _():
            halo_copy(0, c).wait_send()

        @pl.when(me > 0)
        def _():
            halo_copy(1, c).wait_send()

    gone = mem_out.at[pl.ds(0, n - 1)]
    pltpu.make_async_copy(gone, gone, mem_send).wait()
    pltpu.make_async_copy(
        req_out.at[pl.ds(0, n - 1)], req_out.at[pl.ds(0, n - 1)], req_send
    ).wait()


def body(queries, frame_kv, memory_kv, window_offsets, memory_frame, memory_tile):
    frames, rows, columns = queries.shape
    heads = columns // HEAD_DIM
    stored = memory_kv.shape[0]
    n = lax.axis_size("tile")
    kv = jnp.transpose(frame_kv.reshape(frames, rows, 2, heads, HEAD_DIM), (3, 2, 0, 1, 4))
    kv = kv.reshape(heads, 2, frames * rows, HEAD_DIM)
    store = jnp.transpose(
        memory_kv.reshape(stored * TPD, TILE_TOK, 2, heads, HEAD_DIM), (0, 3, 2, 1, 4)
    )
    tokens = frames * rows
    keys = 3 * tokens + n * TILE_TOK
    vmem = pl.BlockSpec(memory_space=pltpu.VMEM)
    smem = pl.BlockSpec(memory_space=pltpu.SMEM)
    dma = pltpu.SemaphoreType.DMA
    return pl.pallas_call(
        functools.partial(kernel, n),
        out_shape=jax.ShapeDtypeStruct(queries.shape, queries.dtype),
        in_specs=[smem, smem, smem, vmem, vmem, vmem],
        out_specs=vmem,
        scratch_shapes=[
            pltpu.VMEM((2, heads, 2, tokens, HEAD_DIM), jnp.bfloat16),
            pltpu.VMEM((n, heads, 2, TILE_TOK, HEAD_DIM), jnp.bfloat16),
            pltpu.VMEM((n, heads, 2, TILE_TOK, HEAD_DIM), jnp.bfloat16),
            pltpu.VMEM((n, 1, 128), jnp.int32),
            pltpu.VMEM((n, 1, 128), jnp.int32),
            pltpu.SMEM((n, 1, 128), jnp.int32),
            pltpu.VMEM((tokens, keys), jnp.float32),
            dma,
            dma,
            dma,
            dma((2, CHUNKS)),
            dma((2, CHUNKS)),
            dma,
            dma((CHUNKS,)),
        ],
        compiler_params=pltpu.CompilerParams(
            collective_id=0, has_side_effects=True, vmem_limit_bytes=56 * 2**20
        ),
        cost_estimate=pl.CostEstimate(
            flops=4 * tokens * keys * columns,
            bytes_accessed=12 * tokens * columns,
            transcendentals=tokens * keys * heads,
        ),
    )(window_offsets, memory_frame, memory_tile, queries, kv, store)


def solution(mesh):
    in_specs = (
        P("groups", "tile", None),
        P("groups", "tile", None, None),
        P("groups", "tile", None, None),
        P("groups"),
        P(("groups", "tile"), None),
        P(("groups", "tile"), None),
    )
    out_specs = P("groups", "tile", None)
    return jax.shard_map(body, mesh=mesh, in_specs=in_specs, out_specs=out_specs, check_vma=False)
```

```python
import functools

import jax
import jax.numpy as jnp
from jax import lax
from jax.experimental import pallas as pl
from jax.experimental.pallas import tpu as pltpu
from jax.sharding import PartitionSpec as P

HEAD_DIM = 128
TILE_TOK = 16
TPD = 3
RADIUS = 3
CHUNKS = 5
OFF = -1e30


def kernel(
    n,
    wo_ref,
    mf_ref,
    mt_ref,
    q_hbm,
    kv_hbm,
    store_hbm,
    out_hbm,
    q_ref,
    out_ref,
    own,
    store,
    halo,
    mem_out,
    mem_in,
    req_out,
    req_in,
    req_now,
    bias,
    req_send,
    req_recv,
    local_sem,
    out_sem,
    halo_send,
    halo_recv,
    mem_send,
    mem_recv,
):
    me = lax.axis_index("tile")
    tokens, heads = kv_hbm.shape[:2]
    frames = q_ref.shape[0]
    rows = TPD * TILE_TOK
    listed = mt_ref.shape[1]
    per = heads // CHUNKS

    def peer_of(k):
        return lax.rem(me + k, n)

    load_store = pltpu.make_async_copy(store_hbm, store, local_sem.at[0])
    load_own = pltpu.make_async_copy(kv_hbm, own, local_sem.at[1])
    load_q = pltpu.make_async_copy(q_hbm, q_ref, local_sem.at[2])
    load_store.start()
    load_own.start()
    load_q.start()

    barrier = pltpu.get_barrier_semaphore()

    @pl.loop(1, n)
    def _(k):
        pl.semaphore_signal(barrier, inc=1, device_id={"tile": peer_of(k)})

    row = lax.broadcasted_iota(jnp.int32, (n, 1, 128), 0)
    wanted = jnp.zeros((n, 1, 128), jnp.int32)
    for a in range(TPD):
        for j in range(listed):
            tile = mt_ref[a, j]
            slot = mf_ref[a, j] * TPD + lax.rem(tile, TPD)
            wanted = jnp.where(row == lax.div(tile, TPD), slot, wanted)
    req_out[...] = wanted

    pl.semaphore_wait(barrier, n - 1)

    def req_copy(k):
        return pltpu.make_async_remote_copy(
            src_ref=req_out.at[peer_of(k)],
            dst_ref=req_in.at[me],
            send_sem=req_send,
            recv_sem=req_recv,
            device_id={"tile": peer_of(k)},
        )

    @pl.loop(1, n)
    def _(k):
        req_copy(k).start()

    def halo_copy(side, c):
        return pltpu.make_async_remote_copy(
            src_ref=kv_hbm.at[:, pl.ds(c * per, per)],
            dst_ref=halo.at[side, c],
            send_sem=halo_send.at[side, c],
            recv_sem=halo_recv.at[side, c],
            device_id={"tile": lax.rem(me + 1, n) if side == 0 else lax.rem(me + n - 1, n)},
        )

    def send_halo(c):
        @pl.when(me < n - 1)
        def _():
            halo_copy(0, c).start()

        @pl.when(me > 0)
        def _():
            halo_copy(1, c).start()

    send_halo(0)

    column = lax.broadcasted_iota(jnp.int32, (TILE_TOK, 3 * tokens), 1)
    source = lax.div(column, tokens)
    local = lax.div(lax.rem(column, rows), TILE_TOK)
    span = local + jnp.where(source == 0, 0, jnp.where(source == 1, -TPD, TPD))
    there = span + me * TPD
    inside = (there >= 0) & (there < n * TPD)
    owner = lax.div(lax.broadcasted_iota(jnp.int32, (TILE_TOK, n * TILE_TOK), 1), TILE_TOK)
    for a in range(TPD):
        hit = jnp.zeros(span.shape, jnp.int32)
        for j in range(wo_ref.shape[0]):
            hit = jnp.where(span - a == wo_ref[j], 1, hit)
        near = jnp.where((hit == 1) & inside, 0.0, OFF)
        got = jnp.zeros(owner.shape, jnp.int32)
        for j in range(listed):
            got = jnp.where(owner == lax.div(mt_ref[a, j], TPD), 1, got)
        far = jnp.where(got == 1, 0.0, OFF)
        for f in range(frames):
            at = pl.ds(f * rows + a * TILE_TOK, TILE_TOK)
            bias[at, : 3 * tokens] = near
            bias[at, 3 * tokens :] = far

    load_store.wait()
    pltpu.make_async_copy(
        req_in.at[pl.ds(0, n - 1)], req_in.at[pl.ds(0, n - 1)], req_recv
    ).wait()
    req_in[me] = req_out[me]
    to_scalar = pltpu.make_async_copy(req_in, req_now, local_sem.at[3])
    to_scalar.start()
    to_scalar.wait()

    def mem_copy(k, c):
        return pltpu.make_async_remote_copy(
            src_ref=mem_out.at[c, peer_of(k)],
            dst_ref=mem_in.at[c, me],
            send_sem=mem_send,
            recv_sem=mem_recv.at[c],
            device_id={"tile": peer_of(k)},
        )

    for c in range(CHUNKS):
        part = pl.ds(c * per, per)
        if c > 0:
            send_halo(c)

        @pl.loop(1, n)
        def _(k):
            mem_out[c, peer_of(k)] = store[req_now[peer_of(k), 0, 0], :, part]
            mem_copy(k, c).start()

        mem_in[c, me] = store[req_now[me, 0, 0], :, part]

    @pl.when(me == 0)
    def _():
        @pl.loop(0, CHUNKS)
        def _(c):
            halo[0, c] = jnp.zeros(halo.shape[2:], halo.dtype)

    @pl.when(me == n - 1)
    def _():
        @pl.loop(0, CHUNKS)
        def _(c):
            halo[1, c] = jnp.zeros(halo.shape[2:], halo.dtype)

    load_own.wait()
    load_q.wait()
    scale = HEAD_DIM**-0.5

    def one_head(c, i):
        h = c * per + i
        at = pl.ds(pl.multiple_of(h * HEAD_DIM, HEAD_DIM), HEAD_DIM)
        q = q_ref[:, :, at].reshape(tokens, HEAD_DIM)
        pairs = [
            own[:, h],
            halo[0, c, :, i],
            halo[1, c, :, i],
            mem_in[c, :, :, i].reshape(n * TILE_TOK, 2, HEAD_DIM),
        ]
        pairs = [jnp.swapaxes(p, 0, 1) for p in pairs]
        keys = jnp.concatenate([p[0] for p in pairs], axis=0)
        values = jnp.concatenate([p[1] for p in pairs], axis=0)
        scores = lax.dot_general(
            q, keys, (((1,), (1,)), ((), ())), preferred_element_type=jnp.float32
        )
        scores = scores * scale + bias[...]
        top = jnp.max(scores, axis=1, keepdims=True)
        terms = jnp.exp(scores - top)
        total = jnp.sum(terms, axis=1, keepdims=True)
        summed = jnp.dot(terms.astype(jnp.bfloat16), values, preferred_element_type=jnp.float32)
        out_ref[:, :, at] = (summed / total).astype(out_ref.dtype).reshape(frames, rows, HEAD_DIM)

    def out_copy(c):
        at = pl.ds(c * per * HEAD_DIM, per * HEAD_DIM)
        return pltpu.make_async_copy(out_ref.at[:, :, at], out_hbm.at[:, :, at], out_sem.at[c])

    for c in range(CHUNKS):

        @pl.when(me > 0)
        def _():
            halo_copy(0, c).wait_recv()

        @pl.when(me < n - 1)
        def _():
            halo_copy(1, c).wait_recv()

        arrived = mem_in.at[c, pl.ds(0, n - 1)]
        pltpu.make_async_copy(arrived, arrived, mem_recv.at[c]).wait()

        @pl.loop(0, per)
        def _(i):
            one_head(c, i)

        out_copy(c).start()

    for c in range(CHUNKS):

        @pl.when(me < n - 1)
        def _():
            halo_copy(0, c).wait_send()

        @pl.when(me > 0)
        def _():
            halo_copy(1, c).wait_send()

    gone = mem_out.at[:, pl.ds(0, n - 1)]
    pltpu.make_async_copy(gone, gone, mem_send).wait()
    pltpu.make_async_copy(
        req_out.at[pl.ds(0, n - 1)], req_out.at[pl.ds(0, n - 1)], req_send
    ).wait()
    for c in range(CHUNKS):
        out_copy(c).wait()


def body(queries, frame_kv, memory_kv, window_offsets, memory_frame, memory_tile):
    frames, rows, columns = queries.shape
    heads = columns // HEAD_DIM
    stored = memory_kv.shape[0] * TPD
    n = lax.axis_size("tile")
    tokens = frames * rows
    keys = 3 * tokens + n * TILE_TOK
    kv = jnp.swapaxes(frame_kv.reshape(tokens, 2, heads, HEAD_DIM), 1, 2)
    store = jnp.swapaxes(memory_kv.reshape(stored, TILE_TOK, 2, heads, HEAD_DIM), 2, 3)
    anywhere = pl.BlockSpec(memory_space=pl.ANY)
    smem = pl.BlockSpec(memory_space=pltpu.SMEM)
    dma = pltpu.SemaphoreType.DMA
    per = heads // CHUNKS
    kept = jnp.bfloat16
    return pl.pallas_call(
        functools.partial(kernel, n),
        out_shape=jax.ShapeDtypeStruct(queries.shape, queries.dtype),
        in_specs=[smem, smem, smem, anywhere, anywhere, anywhere],
        out_specs=anywhere,
        scratch_shapes=[
            pltpu.VMEM(queries.shape, kept),
            pltpu.VMEM(queries.shape, kept),
            pltpu.VMEM(kv.shape, kept),
            pltpu.VMEM(store.shape, kept),
            pltpu.VMEM((2, CHUNKS, tokens, per, 2, HEAD_DIM), kept),
            pltpu.VMEM((CHUNKS, n, TILE_TOK, per, 2, HEAD_DIM), kept),
            pltpu.VMEM((CHUNKS, n, TILE_TOK, per, 2, HEAD_DIM), kept),
            pltpu.VMEM((n, 1, 128), jnp.int32),
            pltpu.VMEM((n, 1, 128), jnp.int32),
            pltpu.SMEM((n, 1, 128), jnp.int32),
            pltpu.VMEM((tokens, keys), jnp.float32),
            dma,
            dma,
            dma((4,)),
            dma((CHUNKS,)),
            dma((2, CHUNKS)),
            dma((2, CHUNKS)),
            dma,
            dma((CHUNKS,)),
        ],
        compiler_params=pltpu.CompilerParams(
            collective_id=0, has_side_effects=True, vmem_limit_bytes=56 * 2**20
        ),
        cost_estimate=pl.CostEstimate(
            flops=4 * tokens * keys * columns,
            bytes_accessed=12 * tokens * columns,
            transcendentals=tokens * keys * heads,
        ),
    )(window_offsets, memory_frame, memory_tile, queries, kv, store)


def solution(mesh):
    in_specs = (
        P("groups", "tile", None),
        P("groups", "tile", None, None),
        P("groups", "tile", None, None),
        P("groups"),
        P(("groups", "tile"), None),
        P(("groups", "tile"), None),
    )
    out_specs = P("groups", "tile", None)
    return jax.shard_map(body, mesh=mesh, in_specs=in_specs, out_specs=out_specs, check_vma=False)
```

```python
import functools

import jax
import jax.numpy as jnp
from jax import lax
from jax.experimental import pallas as pl
from jax.experimental.pallas import tpu as pltpu
from jax.sharding import PartitionSpec as P

HEAD_DIM = 128
TILE_TOK = 16
TPD = 3
RADIUS = 3
CHUNKS = 5
LEAD = 2
OFF = -1e30


def kernel(
    n,
    cornered,
    wo_ref,
    mf_ref,
    mt_ref,
    q_hbm,
    kv_hbm,
    store_hbm,
    out_hbm,
    q_ref,
    out_ref,
    own,
    store,
    halo,
    relay,
    mem_out,
    mem_in,
    req_out,
    req_in,
    req_now,
    bias,
    req_send,
    req_recv,
    local_sem,
    out_sem,
    halo_send,
    halo_recv,
    relay_recv,
    relay_send,
    mem_send,
    mem_recv,
):
    me = lax.axis_index("tile")
    frames, rows, heads = kv_hbm.shape[:3]
    tokens = frames * rows
    listed = mt_ref.shape[1]
    per = heads // CHUNKS

    def peer_of(k):
        return lax.rem(me + k, n)

    load_store = pltpu.make_async_copy(store_hbm, store, local_sem.at[0])
    load_own = pltpu.make_async_copy(kv_hbm, own, local_sem.at[1])
    load_q = pltpu.make_async_copy(q_hbm, q_ref, local_sem.at[2])
    load_store.start()
    load_own.start()
    load_q.start()

    barrier = pltpu.get_barrier_semaphore()

    @pl.loop(1, n)
    def _(k):
        pl.semaphore_signal(barrier, inc=1, device_id={"tile": peer_of(k)})

    row = lax.broadcasted_iota(jnp.int32, (n, 1, 128), 0)
    wanted = jnp.zeros((n, 1, 128), jnp.int32)
    for a in range(TPD):
        for j in range(listed):
            tile = mt_ref[a, j]
            slot = mf_ref[a, j] * TPD + lax.rem(tile, TPD)
            wanted = jnp.where(row == lax.div(tile, TPD), slot, wanted)
    req_out[...] = wanted

    pl.semaphore_wait(barrier, n - 1)

    def req_copy(k):
        return pltpu.make_async_remote_copy(
            src_ref=req_out.at[peer_of(k)],
            dst_ref=req_in.at[me],
            send_sem=req_send,
            recv_sem=req_recv,
            device_id={"tile": peer_of(k)},
        )

    @pl.loop(1, n)
    def _(k):
        req_copy(k).start()

    exists = (me < n - 1, me > 0)
    missing = (me == 0, me == n - 1)
    level, place, levels = lax.div(me, 4), lax.rem(me, 4), n // 4
    relayed = (lax.div(frames * (levels - 1 - level), levels), lax.div(frames * level, levels))
    round_corner = (place == 3, place == 0)
    is_relay = ((place == 0) & (me + 4 < n), (place == 3) & (me >= 4))

    def halo_copy(side, c, f, by_relay):
        to = (-3 if by_relay else 1) * (1 if side == 0 else -1)
        return pltpu.make_async_remote_copy(
            src_ref=kv_hbm.at[f, :, pl.ds(c * per, per)],
            dst_ref=relay.at[c, f] if by_relay else halo.at[side, c, f],
            send_sem=halo_send.at[side],
            recv_sem=relay_recv.at[c, f] if by_relay else halo_recv.at[side, c],
            device_id={"tile": lax.rem(me + to + n, n)},
        )

    def forward_copy(side, c, f):
        return pltpu.make_async_remote_copy(
            src_ref=relay.at[c, f],
            dst_ref=halo.at[side, c, f],
            send_sem=relay_send.at[c, f],
            recv_sem=halo_recv.at[side, c],
            device_id={"tile": lax.rem(me + (4 if side == 0 else -4) + n, n)},
        )

    def send_halo(c, by_relay):
        for side in range(2):
            for f in range(frames):
                if not cornered:
                    go = None if by_relay else exists[side]
                else:
                    via = round_corner[side] & (f < relayed[side])
                    go = exists[side] & (via if by_relay else ~via)
                    if by_relay and f == frames - 1:
                        go = None
                if go is not None:

                    @pl.when(go)
                    def _():
                        halo_copy(side, c, f, by_relay).start()

    def at_relay(c, act):
        if cornered:
            for side in range(2):
                for f in range(frames - 1):

                    @pl.when(is_relay[side] & (f < relayed[side]))
                    def _():
                        act(side, c, f)

    def forward(side, c, f):
        halo_copy(side, c, f, True).wait_recv()
        forward_copy(side, c, f).start()

    for c in range(LEAD):
        send_halo(c, True)
    send_halo(0, False)

    column = lax.broadcasted_iota(jnp.int32, (TILE_TOK, 3 * tokens), 1)
    source = lax.div(column, tokens)
    local = lax.div(lax.rem(column, rows), TILE_TOK)
    span = local + jnp.where(source == 0, 0, jnp.where(source == 1, -TPD, TPD))
    there = span + me * TPD
    inside = (there >= 0) & (there < n * TPD)
    owner = lax.div(lax.broadcasted_iota(jnp.int32, (TILE_TOK, n * TILE_TOK), 1), TILE_TOK)
    for a in range(TPD):
        hit = jnp.zeros(span.shape, jnp.int32)
        for j in range(wo_ref.shape[0]):
            hit = jnp.where(span - a == wo_ref[j], 1, hit)
        near = jnp.where((hit == 1) & inside, 0.0, OFF)
        got = jnp.zeros(owner.shape, jnp.int32)
        for j in range(listed):
            got = jnp.where(owner == lax.div(mt_ref[a, j], TPD), 1, got)
        far = jnp.where(got == 1, 0.0, OFF)
        for f in range(frames):
            at = pl.ds(f * rows + a * TILE_TOK, TILE_TOK)
            bias[at, : 3 * tokens] = near
            bias[at, 3 * tokens :] = far

    load_store.wait()
    pltpu.make_async_copy(
        req_in.at[pl.ds(0, n - 1)], req_in.at[pl.ds(0, n - 1)], req_recv
    ).wait()
    req_in[me] = req_out[me]
    to_scalar = pltpu.make_async_copy(req_in, req_now, local_sem.at[3])
    to_scalar.start()
    to_scalar.wait()

    def mem_copy(k, c):
        return pltpu.make_async_remote_copy(
            src_ref=mem_out.at[c, peer_of(k)],
            dst_ref=mem_in.at[c, me],
            send_sem=mem_send,
            recv_sem=mem_recv.at[c],
            device_id={"tile": peer_of(k)},
        )

    for c in range(CHUNKS):
        part = pl.ds(c * per, per)
        if c + LEAD < CHUNKS:
            send_halo(c + LEAD, True)
        if c > 0:
            send_halo(c, False)

        @pl.loop(1, n)
        def _(k):
            mem_out[c, peer_of(k)] = store[req_now[peer_of(k), 0, 0], :, part]
            mem_copy(k, c).start()

        mem_in[c, me] = store[req_now[me, 0, 0], :, part]

    for side in range(2):

        @pl.when(missing[side])
        def _():
            @pl.loop(0, CHUNKS)
            def _(c):
                halo[side, c] = jnp.zeros(halo.shape[2:], halo.dtype)

    at_relay(0, forward)
    load_own.wait()
    load_q.wait()
    scale = HEAD_DIM**-0.5

    def one_head(c, i):
        h = c * per + i
        at = pl.ds(pl.multiple_of(h * HEAD_DIM, HEAD_DIM), HEAD_DIM)
        q = q_ref[:, :, at].reshape(tokens, HEAD_DIM)
        pairs = [
            own[:, :, h].reshape(tokens, 2, HEAD_DIM),
            halo[0, c, :, :, i].reshape(tokens, 2, HEAD_DIM),
            halo[1, c, :, :, i].reshape(tokens, 2, HEAD_DIM),
            mem_in[c, :, :, i].reshape(n * TILE_TOK, 2, HEAD_DIM),
        ]
        pairs = [jnp.swapaxes(p, 0, 1) for p in pairs]
        keys = jnp.concatenate([p[0] for p in pairs], axis=0)
        values = jnp.concatenate([p[1] for p in pairs], axis=0)
        scores = lax.dot_general(
            q, keys, (((1,), (1,)), ((), ())), preferred_element_type=jnp.float32
        )
        scores = scores * scale + bias[...]
        top = jnp.max(scores, axis=1, keepdims=True)
        terms = jnp.exp(scores - top)
        total = jnp.sum(terms, axis=1, keepdims=True)
        summed = jnp.dot(terms.astype(jnp.bfloat16), values, preferred_element_type=jnp.float32)
        out_ref[:, :, at] = (summed / total).astype(out_ref.dtype).reshape(frames, rows, HEAD_DIM)

    def out_copy(c):
        at = pl.ds(c * per * HEAD_DIM, per * HEAD_DIM)
        return pltpu.make_async_copy(out_ref.at[:, :, at], out_hbm.at[:, :, at], out_sem.at[c])

    for c in range(CHUNKS):
        if c + 1 < CHUNKS:
            at_relay(c + 1, forward)

        for side in range(2):

            @pl.when(~missing[side])
            def _():
                arrived = halo.at[side, c]
                pltpu.make_async_copy(arrived, arrived, halo_recv.at[side, c]).wait()

        arrived = mem_in.at[c, pl.ds(0, n - 1)]
        pltpu.make_async_copy(arrived, arrived, mem_recv.at[c]).wait()

        @pl.loop(0, per)
        def _(i):
            one_head(c, i)

        out_copy(c).start()

    for side in range(2):

        @pl.when(exists[side])
        def _():
            gone = halo.at[side]
            pltpu.make_async_copy(gone, gone, halo_send.at[side]).wait()

    for c in range(CHUNKS):
        at_relay(c, lambda side, c, f: forward_copy(side, c, f).wait_send())
    gone = mem_out.at[:, pl.ds(0, n - 1)]
    pltpu.make_async_copy(gone, gone, mem_send).wait()
    pltpu.make_async_copy(
        req_out.at[pl.ds(0, n - 1)], req_out.at[pl.ds(0, n - 1)], req_send
    ).wait()
    for c in range(CHUNKS):
        out_copy(c).wait()


def body(cornered, queries, frame_kv, memory_kv, window_offsets, memory_frame, memory_tile):
    frames, rows, columns = queries.shape
    heads = columns // HEAD_DIM
    stored = memory_kv.shape[0] * TPD
    n = lax.axis_size("tile")
    tokens = frames * rows
    keys = 3 * tokens + n * TILE_TOK
    kv = jnp.swapaxes(frame_kv.reshape(frames, rows, 2, heads, HEAD_DIM), 2, 3)
    store = jnp.swapaxes(memory_kv.reshape(stored, TILE_TOK, 2, heads, HEAD_DIM), 2, 3)
    anywhere = pl.BlockSpec(memory_space=pl.ANY)
    smem = pl.BlockSpec(memory_space=pltpu.SMEM)
    dma = pltpu.SemaphoreType.DMA
    per = heads // CHUNKS
    kept = jnp.bfloat16
    return pl.pallas_call(
        functools.partial(kernel, n, cornered),
        out_shape=jax.ShapeDtypeStruct(queries.shape, queries.dtype),
        in_specs=[smem, smem, smem, anywhere, anywhere, anywhere],
        out_specs=anywhere,
        scratch_shapes=[
            pltpu.VMEM(queries.shape, kept),
            pltpu.VMEM(queries.shape, kept),
            pltpu.VMEM(kv.shape, kept),
            pltpu.VMEM(store.shape, kept),
            pltpu.VMEM((2, CHUNKS, frames, rows, per, 2, HEAD_DIM), kept),
            pltpu.VMEM((CHUNKS, frames - 1, rows, per, 2, HEAD_DIM), kept),
            pltpu.VMEM((CHUNKS, n, TILE_TOK, per, 2, HEAD_DIM), kept),
            pltpu.VMEM((CHUNKS, n, TILE_TOK, per, 2, HEAD_DIM), kept),
            pltpu.VMEM((n, 1, 128), jnp.int32),
            pltpu.VMEM((n, 1, 128), jnp.int32),
            pltpu.SMEM((n, 1, 128), jnp.int32),
            pltpu.VMEM((tokens, keys), jnp.float32),
            dma,
            dma,
            dma((4,)),
            dma((CHUNKS,)),
            dma((2,)),
            dma((2, CHUNKS)),
            dma((CHUNKS, frames - 1)),
            dma((CHUNKS, frames - 1)),
            dma,
            dma((CHUNKS,)),
        ],
        compiler_params=pltpu.CompilerParams(
            collective_id=0, has_side_effects=True, vmem_limit_bytes=56 * 2**20
        ),
        cost_estimate=pl.CostEstimate(
            flops=4 * tokens * keys * columns,
            bytes_accessed=12 * tokens * columns,
            transcendentals=tokens * keys * heads,
        ),
    )(window_offsets, memory_frame, memory_tile, queries, kv, store)


def has_corners(mesh):
    line = mesh.devices[0]
    if mesh.axis_names != ("groups", "tile") or len(line) % 4 or len(line) < 8:
        return False
    spots = [d.coords for d in line]

    def apart(i, j):
        return sum(p != q for p, q in zip(spots[i], spots[j]))

    whole = range(0, len(line), 4)
    return all(
        apart(i, i + 1) == 0 and apart(i + 2, i + 3) == 0 and apart(i, i + 2) == 1 for i in whole
    ) and all(apart(i - 1, i) == 2 and apart(i - 4, i) == 1 for i in whole[1:])


def solution(mesh):
    in_specs = (
        P("groups", "tile", None),
        P("groups", "tile", None, None),
        P("groups", "tile", None, None),
        P("groups"),
        P(("groups", "tile"), None),
        P(("groups", "tile"), None),
    )
    out_specs = P("groups", "tile", None)
    return jax.shard_map(
        functools.partial(body, has_corners(mesh)), mesh=mesh, in_specs=in_specs, out_specs=out_specs, check_vma=False
    )
```
